32 devices in a mesh: hi: 8 (over z, x), lo: 4 (over y, core).
Axes of the slice: x: 2, y: 2, z: 4, core: 2. Of those that a mesh axis runs over, the one named last changes fastest.
Arguments:
- sources: bfloat16 [64, 524288], P(None, ('hi', 'lo')), may hold values from -6 to 6
- leaf_in: bfloat16 [2048, 64, 256], P(('hi', 'lo')), may hold values from -0.375 to 0.375
- local_mix: bfloat16 [2048, 6, 64, 128], P(('hi', 'lo')), may hold values from -0.5 to 0.5
- lo_mix: bfloat16 [2048, 2, 64, 128], P(('hi', 'lo')), may hold values from -0.5 to 0.5
- hi_mix: bfloat16 [2048, 3, 64, 128], P(('hi', 'lo')), may hold values from -0.5 to 0.5
- leaf_out: bfloat16 [2048, 64, 256], P(('hi', 'lo')), may hold values from -0.75 to 0.75
Outputs:
- targets: bfloat16 [64, 524288], P(None, ('hi', 'lo'))
The draws below stay inside these ranges and needn't reach their ends.
All inputs are finite; a program needn't handle non-finite values.
Results may differ from the reference program's by a relative error of at most 0.029.
Values may be sent and summed in bfloat16 or wider, within the bound.
No kernel may reach another device: no remote copies, remote signals or barrier semaphores. Data moves between devices by JAX's collectives and lax.ppermute only.
A program may use at most 128 MiB of HBM per device.

```python
import jax
import jax.numpy as jnp

RANK = 64
LEAF = 256
VECS = 64
LOC_LEV = 6
LO_BITS = 2
HI_BITS = 3
BLOCKS = 2048
POINTS = 524288


def level_of(stream_key, shape, cuts, low, largest):
    def one(position, blocks):
        draws = jax.random.uniform(jax.random.fold_in(jax.random.fold_in(stream_key, 6), position), (blocks,), jnp.float32, low / len(cuts), largest / len(cuts))
        return jnp.repeat(jnp.exp(draws), shape[position] // blocks).reshape((-1,) + (1,) * (len(shape) - position - 1))

    loudness = one(*cuts[0])
    for cut in cuts[1:]:
        loudness = loudness * one(*cut)
    return loudness


def gaussian(key, dims, scale, limit, split=(), kind=jnp.bfloat16):
    array = jax.random.normal(key, dims, jnp.float32) * scale
    if len(split) > 0:
        array = level_of(key, dims, split, -0.22, 0.18) * array
    return jnp.clip(array, min=-limit, max=limit).astype(kind)


def setup_inputs(seed: int = 0) -> dict:
    seeds = jax.random.split(jax.random.key(seed), 7)
    return {
        "sources": gaussian(seeds[0], (VECS, POINTS), 1.0, 6.0, ((1, 32),)),
        "leaf_in": gaussian(seeds[1], (BLOCKS, RANK, LEAF), LEAF ** -0.5, 0.375, ((0, 32),)),
        "local_mix": gaussian(seeds[2], (BLOCKS, LOC_LEV, RANK, 2 * RANK), (2 * RANK) ** -0.5, 0.5, ((0, 32),)),
        "lo_mix": gaussian(seeds[3], (BLOCKS, LO_BITS, RANK, 2 * RANK), (2 * RANK) ** -0.5, 0.5, ((0, 32),)),
        "hi_mix": gaussian(seeds[4], (BLOCKS, HI_BITS, RANK, 2 * RANK), (2 * RANK) ** -0.5, 0.5, ((0, 32),)),
        "leaf_out": gaussian(seeds[5], (BLOCKS, RANK, LEAF), RANK ** -0.5, 0.75, ((0, 32),)),
    }


def flip_blocks(current, level_bit):
    shape_now = current.shape
    grouped = current.reshape((shape_now[0] >> (level_bit + 1), 2, 1 << level_bit) + shape_now[1:])
    return grouped[:, ::-1].reshape(shape_now)


def mix_level(current, partner, factors):
    joined = jnp.concatenate([current, partner], axis=-1).astype(jnp.float32)
    mixed = jnp.einsum("kvs,kqs->kvq", joined, factors.astype(jnp.float32))
    return mixed.astype(jnp.bfloat16)


def reference(sources, leaf_in, local_mix, lo_mix, hi_mix, leaf_out):
    blocks_all = leaf_in.shape[0]
    leaf_size = leaf_in.shape[2]
    vectors = sources.shape[0]
    source_blocks = sources.reshape(vectors, blocks_all, leaf_size).astype(jnp.float32)
    current = jnp.einsum("vkl,krl->kvr", source_blocks, leaf_in.astype(jnp.float32)).astype(jnp.bfloat16)
    level_bit = 0
    for level in range(LOC_LEV):
        current = mix_level(current, flip_blocks(current, level_bit), local_mix[:, level])
        level_bit = level_bit + 1
    for level in range(LO_BITS):
        current = mix_level(current, flip_blocks(current, level_bit), lo_mix[:, level])
        level_bit = level_bit + 1
    for level in range(HI_BITS):
        current = mix_level(current, flip_blocks(current, level_bit), hi_mix[:, level])
        level_bit = level_bit + 1
    result = jnp.einsum("kvr,krl->vkl", current.astype(jnp.float32), leaf_out.astype(jnp.float32))
    return result.reshape(vectors, blocks_all * leaf_size).astype(jnp.bfloat16)
```

```python
import functools

import jax
import jax.numpy as jnp
from jax import lax
from jax.experimental import pallas as pl
from jax.experimental.pallas import tpu as pltpu
from jax.sharding import PartitionSpec as P

NT = (((1,), (1,)), ((), ()))
PIECES = 4
SHARES = (5, 9, 10, 8)
LAGS = (
    (1.0, 1.1, 1.2, 1.3),
    (0.0, 0.5, 1.2, 1.6),
    (0.0, 0.5, 1.1, 1.6),
    (0.0, 0.5, 1.2, 2.15),
    (0.0, 0.9, 1.1, 2.1),
)


def half_swap(x):
    half = x.shape[1] // 2
    return jnp.concatenate([x[:, half:], x[:, :half]], axis=1)


def pack(product):
    rows = product.shape[0] // 2
    top, bottom = product[:rows], product[rows:]
    low = lax.broadcasted_iota(jnp.int32, top.shape, 1) < top.shape[1] // 2
    return jnp.where(low, top, bottom)


def mix_pair(own, other, factors):
    joined = jnp.concatenate([own, other], axis=0)
    rows, width = factors.shape[1:]
    product = jnp.dot(
        factors.reshape(2 * rows, width), joined, preferred_element_type=jnp.float32
    )
    return pack(product)


def local_kernel(
    src_hbm,
    leaf_hbm,
    mix_hbm,
    lo_hbm,
    first,
    state,
    last_mix,
    lo_mix,
    even,
    odd,
    src,
    leaf,
    mix,
    src_sem,
    leaf_sem,
    mix_sem,
    lo_sem,
):
    pairs = even.shape[0]
    blocks = leaf.shape[0]
    levels = mix_hbm.shape[1]
    width = leaf.shape[2]

    def inputs(piece):
        count = blocks // PIECES
        cols = pl.ds(piece * count * width, count * width)
        rows = pl.ds(piece * count, count)
        return (
            pltpu.make_async_copy(src_hbm.at[:, cols], src.at[:, cols], src_sem.at[piece]),
            pltpu.make_async_copy(leaf_hbm.at[rows], leaf.at[rows], leaf_sem.at[piece]),
        )

    def factors(level):
        held = mix.at[level] if level < levels - 1 else last_mix
        return pltpu.make_async_copy(mix_hbm.at[:, level], held, mix_sem.at[level])

    next_levels = pltpu.make_async_copy(lo_hbm, lo_mix, lo_sem)
    for piece in range(PIECES):
        for copy in inputs(piece):
            copy.start()

    queue = [factors(level) for level in range(levels)]
    for piece in range(PIECES):
        for copy in inputs(piece):
            copy.wait()
        for copy in queue[piece * levels // PIECES : (piece + 1) * levels // PIECES]:
            copy.start()
        for pair in range(piece * pairs // PIECES, (piece + 1) * pairs // PIECES):
            columns = [src[:, pl.ds((2 * pair + side) * width, width)] for side in range(2)]
            product = lax.dot_general(
                leaf[2 * pair : 2 * pair + 2].reshape(-1, width),
                jnp.concatenate(columns, axis=0),
                NT,
                preferred_element_type=jnp.float32,
            )
            even[pair] = pack(product).astype(even.dtype)
    next_levels.start()

    for level in range(levels):
        factors(level).wait()
        old, new = (odd, even) if level % 2 else (even, odd)
        if level == levels - 2:
            new = state
        if level == levels - 1:
            old, new = state, first
        for pair in range(new.shape[0]):
            own = old[pair]
            other = half_swap(own) if level == 0 else old[pair ^ 1 << level - 1]
            chosen = last_mix if level == levels - 1 else mix.at[level]
            part = chosen[2 * pair : 2 * pair + 2]
            new[pair] = mix_pair(own, other, part).astype(own.dtype)
    next_levels.wait()


def local_phase(sources, leaf_in, local_mix, lo_mix, size):
    vectors = sources.shape[0]
    blocks, rank, _ = leaf_in.shape
    levels = local_mix.shape[1]
    return pl.pallas_call(
        local_kernel,
        out_shape=[
            pltpu.VMEM((size, rank, 2 * vectors), jnp.bfloat16),
            pltpu.VMEM((blocks // 2, rank, 2 * vectors), jnp.bfloat16),
            pltpu.VMEM((blocks,) + local_mix.shape[2:], local_mix.dtype),
            pltpu.VMEM(lo_mix.shape, lo_mix.dtype),
        ],
        in_specs=[pl.BlockSpec(memory_space=pltpu.HBM)] * 4,
        out_specs=[pl.BlockSpec(memory_space=pltpu.VMEM)] * 4,
        scratch_shapes=[
            pltpu.VMEM((blocks // 2, rank, 2 * vectors), jnp.bfloat16),
            pltpu.VMEM((blocks // 2, rank, 2 * vectors), jnp.bfloat16),
            pltpu.VMEM(sources.shape, sources.dtype),
            pltpu.VMEM(leaf_in.shape, leaf_in.dtype),
            pltpu.VMEM((levels - 1, blocks) + local_mix.shape[2:], local_mix.dtype),
            pltpu.SemaphoreType.DMA((PIECES,)),
            pltpu.SemaphoreType.DMA((PIECES,)),
            pltpu.SemaphoreType.DMA((levels,)),
            pltpu.SemaphoreType.DMA,
        ],
        compiler_params=pltpu.CompilerParams(vmem_limit_bytes=58 << 20),
        cost_estimate=pl.CostEstimate(flops=10**9, bytes_accessed=10 << 20, transcendentals=0),
        name="local_levels",
    )(sources, leaf_in, local_mix, lo_mix)


def rest_kernel(start, state_ref, mix_ref, after_ref, out_ref):
    pairs = state_ref.shape[0]
    for p in range(out_ref.shape[0]):
        pair = start + p
        other = state_ref[pair ^ pairs // 2]
        mixed = mix_pair(state_ref[pair], other, mix_ref[2 * pair : 2 * pair + 2])
        out_ref[p] = mixed.astype(out_ref.dtype)


def local_rest(state, last_mix, start, stop, after):
    _, rank, lanes = state.shape
    return pl.pallas_call(
        functools.partial(rest_kernel, start),
        out_shape=pltpu.VMEM((stop - start, rank, lanes), state.dtype),
        in_specs=[pl.BlockSpec(memory_space=pltpu.VMEM)] * 2 + [pl.BlockSpec(memory_space=pl.ANY)],
        out_specs=pl.BlockSpec(memory_space=pltpu.VMEM),
        compiler_params=pltpu.CompilerParams(vmem_limit_bytes=8 << 20),
        cost_estimate=pl.CostEstimate(flops=3 * 10**9, bytes_accessed=0, transcendentals=0),
        name="local_rest",
    )(state, last_mix, after)


def cross_kernel(level, start, offset, own_ref, other_ref, mix_ref, after_ref, out_ref):
    for p in range(out_ref.shape[0]):
        block = 2 * (start + p)
        mixed = mix_pair(
            own_ref[offset + p], other_ref[offset + p], mix_ref[block : block + 2, level]
        )
        out_ref[p] = mixed.astype(out_ref.dtype)


def cross_level(own, other, mix, level, start, offset, size, after):
    _, rank, lanes = own.shape
    return pl.pallas_call(
        functools.partial(cross_kernel, level, start, offset),
        out_shape=pltpu.VMEM((size, rank, lanes), own.dtype),
        in_specs=[pl.BlockSpec(memory_space=pltpu.VMEM)] * 3 + [pl.BlockSpec(memory_space=pl.ANY)],
        out_specs=pl.BlockSpec(memory_space=pltpu.VMEM),
        compiler_params=pltpu.CompilerParams(vmem_limit_bytes=8 << 20),
        cost_estimate=pl.CostEstimate(flops=3 * 10**9, bytes_accessed=0, transcendentals=0),
        name="cross_level",
    )(own, other, mix, after)


def final_kernel(has_token, level, start, own_ref, other_ref, mix_ref, leaf_ref, *rest):
    out_hbm, *tokens, held, sem = rest[-4 if has_token else -3 :]
    for token in tokens:
        token[...] = jnp.zeros_like(token)
    pairs = own_ref.shape[0]
    vectors = held.shape[0]
    width = leaf_ref.shape[2]
    turned = []
    for p in range(pairs):
        block = 2 * (start + p)
        mixed = mix_pair(own_ref[p], other_ref[p], mix_ref[block : block + 2, level])
        turned.append(mixed.astype(jnp.bfloat16).T)
    copies = []
    for first, stop in ((0, pairs // 2), (pairs // 2, pairs)):
        for p in range(first, stop):
            for side in range(2):
                held[:, pl.ds((2 * p + side) * width, width)] = jnp.dot(
                    turned[p][side * vectors : (side + 1) * vectors],
                    leaf_ref[2 * (start + p) + side],
                    preferred_element_type=jnp.float32,
                ).astype(held.dtype)
        count = 2 * (stop - first) * width
        copies.append(
            pltpu.make_async_copy(
                held.at[:, pl.ds(2 * first * width, count)],
                out_hbm.at[:, pl.ds(2 * (start + first) * width, count)],
                sem.at[len(copies)],
            )
        )
        copies[-1].start()
    for copy in copies:
        copy.wait()


def final_level(own, other, mix, leaf_out, level, start, so_far, after, has_token):
    blocks, rank, width = leaf_out.shape
    pairs, _, lanes = own.shape
    vectors = lanes // 2
    in_specs = [pl.BlockSpec(memory_space=pltpu.VMEM)] * 4 + [pl.BlockSpec(memory_space=pl.ANY)]
    operands = [own, other, mix, leaf_out, after]
    aliases = {}
    if so_far is not None:
        in_specs.append(pl.BlockSpec(memory_space=pltpu.HBM))
        operands.append(so_far)
        aliases = {5: 0}
    return pl.pallas_call(
        functools.partial(final_kernel, has_token, level, start),
        out_shape=[jax.ShapeDtypeStruct((vectors, blocks * width), own.dtype)]
        + [pltpu.VMEM((8, lanes), jnp.float32)] * has_token,
        in_specs=in_specs,
        out_specs=[pl.BlockSpec(memory_space=pltpu.HBM)]
        + [pl.BlockSpec(memory_space=pltpu.VMEM)] * has_token,
        scratch_shapes=[
            pltpu.VMEM((vectors, 2 * pairs * width), own.dtype),
            pltpu.SemaphoreType.DMA((2,)),
        ],
        input_output_aliases=aliases,
        compiler_params=pltpu.CompilerParams(vmem_limit_bytes=8 << 20),
        cost_estimate=pl.CostEstimate(flops=3 * 10**9, bytes_accessed=0, transcendentals=0),
        name="final_level",
    )(*operands)


def swapped(block, axis, stride):
    count = lax.axis_size(axis)
    route = [(i, i ^ (1 << stride)) for i in range(count)]
    return lax.ppermute(block, axis, route)


def cut(total, shares):
    ends = [total * sum(shares[: c + 1]) // sum(shares) for c in range(len(shares))]
    return list(zip([0] + ends[:-1], ends))


def body(sources, leaf_in, local_mix, lo_mix, hi_mix, leaf_out):
    lo_levels = lax.axis_size("lo").bit_length() - 1
    hi_levels = lax.axis_size("hi").bit_length() - 1
    pairs = leaf_in.shape[0] // 2
    steps = [("lo", n, lo_mix) for n in range(lo_levels)]
    steps += [("hi", n, hi_mix) for n in range(hi_levels)]
    end = len(steps) - 1
    parts = cut(pairs, SHARES)
    head = parts[0][1]
    waiting = {}

    def turn(item):
        s, c = item
        lags = LAGS[min(end - s, 3) if s else 4]
        return s + lags[c], -s

    first, state, last_mix, lo_mix = local_phase(sources, leaf_in, local_mix, lo_mix, head)
    steps[:lo_levels] = [("lo", n, lo_mix) for n in range(lo_levels)]
    axis, level, _ = steps[0]
    waiting[0, 0] = first, swapped(first, axis, level), 0
    after = state
    targets = None
    for s, c in sorted(((s, c) for s in range(end + 1) for c in range(len(parts))), key=turn):
        own, other, offset = waiting.pop((s, c))
        _, level, mix = steps[s]
        start, stop = parts[c]
        if s == end:
            more = c < len(parts) - 1
            targets, *tokens = final_level(
                own, other, mix, leaf_out, level, start, targets, after, more
            )
            after = tokens[0] if more else None
            continue
        block = after = cross_level(own, other, mix, level, start, offset, stop - start, after)
        if s == 0 and c == 0:
            after = local_rest(state, last_mix, *parts[1], after)
            waiting[0, 1] = after, swapped(after, *steps[0][:2]), 0
        if s == 0 and c == 1:
            after = rest = local_rest(state, last_mix, stop, pairs, after)
            partner = swapped(rest, *steps[0][:2])
            for d in range(2, len(parts)):
                waiting[0, d] = rest, partner, parts[d][0] - stop
        axis, level, _ = steps[s + 1]
        waiting[s + 1, c] = block, swapped(block, axis, level), 0
    return targets


def solution(mesh):
    return jax.shard_map(
        body,
        mesh=mesh,
        in_specs=(
            P(None, ("hi", "lo")),
            P(("hi", "lo"), None, None),
            P(("hi", "lo"), None, None, None),
            P(("hi", "lo"), None, None, None),
            P(("hi", "lo"), None, None, None),
            P(("hi", "lo"), None, None),
        ),
        out_specs=P(None, ("hi", "lo")),
        check_vma=False,
    )
```

```python
import functools

import jax
import jax.numpy as jnp
from jax import lax
from jax.experimental import pallas as pl
from jax.experimental.pallas import tpu as pltpu
from jax.sharding import PartitionSpec as P

NT = (((1,), (1,)), ((), ()))
PIECES = 8
SHARES = (5, 8, 10, 9)
LAGS = (
    (1.0, 1.1, 1.2, 1.3),
    (0.0, 0.5, 1.2, 1.6),
    (0.0, 0.5, 1.1, 1.6),
    (0.0, 0.5, 1.2, 2.15),
    (0.0, 0.9, 1.1, 2.1),
)


def half_swap(x):
    half = x.shape[1] // 2
    return jnp.concatenate([x[:, half:], x[:, :half]], axis=1)


def pack(product):
    rows = product.shape[0] // 2
    top, bottom = product[:rows], product[rows:]
    low = lax.broadcasted_iota(jnp.int32, top.shape, 1) < top.shape[1] // 2
    return jnp.where(low, top, bottom)


def mix_pair(own, other, factors):
    joined = jnp.concatenate([own, other], axis=0)
    rows, width = factors.shape[1:]
    product = jnp.dot(
        factors.reshape(2 * rows, width), joined, preferred_element_type=jnp.float32
    )
    return pack(product)


def local_kernel(
    src_hbm,
    leaf_hbm,
    mix_hbm,
    first,
    state,
    last_mix,
    even,
    odd,
    src,
    leaf,
    mix,
    src_sem,
    leaf_sem,
    mix_sem,
):
    pairs = even.shape[0]
    blocks = leaf.shape[0]
    levels = mix_hbm.shape[1]
    width = leaf.shape[2]

    def inputs(piece):
        count = blocks // PIECES
        cols = pl.ds(piece * count * width, count * width)
        rows = pl.ds(piece * count, count)
        return (
            pltpu.make_async_copy(src_hbm.at[:, cols], src.at[:, cols], src_sem.at[piece]),
            pltpu.make_async_copy(leaf_hbm.at[rows], leaf.at[rows], leaf_sem.at[piece]),
        )

    def factors(level):
        held = mix.at[level] if level < levels - 1 else last_mix
        return pltpu.make_async_copy(mix_hbm.at[:, level], held, mix_sem.at[level])

    for piece in range(PIECES):
        for copy in inputs(piece):
            copy.start()

    queue = [factors(level) for level in range(levels)]
    for piece in range(PIECES):
        for copy in inputs(piece):
            copy.wait()
        for copy in queue[piece * levels // PIECES : (piece + 1) * levels // PIECES]:
            copy.start()
        for pair in range(piece * pairs // PIECES, (piece + 1) * pairs // PIECES):
            columns = [src[:, pl.ds((2 * pair + side) * width, width)] for side in range(2)]
            product = lax.dot_general(
                leaf[2 * pair : 2 * pair + 2].reshape(-1, width),
                jnp.concatenate(columns, axis=0),
                NT,
                preferred_element_type=jnp.float32,
            )
            even[pair] = pack(product).astype(even.dtype)

    for level in range(levels):
        factors(level).wait()
        old, new = (odd, even) if level % 2 else (even, odd)
        if level == levels - 2:
            new = state
        if level == levels - 1:
            old, new = state, first
        for pair in range(new.shape[0]):
            own = old[pair]
            other = half_swap(own) if level == 0 else old[pair ^ 1 << level - 1]
            chosen = last_mix if level == levels - 1 else mix.at[level]
            part = chosen[2 * pair : 2 * pair + 2]
            new[pair] = mix_pair(own, other, part).astype(own.dtype)


def local_phase(sources, leaf_in, local_mix, size):
    vectors = sources.shape[0]
    blocks, rank, _ = leaf_in.shape
    levels = local_mix.shape[1]
    return pl.pallas_call(
        local_kernel,
        out_shape=[
            pltpu.VMEM((size, rank, 2 * vectors), jnp.bfloat16),
            pltpu.VMEM((blocks // 2, rank, 2 * vectors), jnp.bfloat16),
            pltpu.VMEM((blocks,) + local_mix.shape[2:], local_mix.dtype),
        ],
        in_specs=[pl.BlockSpec(memory_space=pltpu.HBM)] * 3,
        out_specs=[pl.BlockSpec(memory_space=pltpu.VMEM)] * 3,
        scratch_shapes=[
            pltpu.VMEM((blocks // 2, rank, 2 * vectors), jnp.bfloat16),
            pltpu.VMEM((blocks // 2, rank, 2 * vectors), jnp.bfloat16),
            pltpu.VMEM(sources.shape, sources.dtype),
            pltpu.VMEM(leaf_in.shape, leaf_in.dtype),
            pltpu.VMEM((levels - 1, blocks) + local_mix.shape[2:], local_mix.dtype),
            pltpu.SemaphoreType.DMA((PIECES,)),
            pltpu.SemaphoreType.DMA((PIECES,)),
            pltpu.SemaphoreType.DMA((levels,)),
        ],
        compiler_params=pltpu.CompilerParams(vmem_limit_bytes=58 << 20),
        cost_estimate=pl.CostEstimate(flops=10**9, bytes_accessed=10 << 20, transcendentals=0),
        name="local_levels",
    )(sources, leaf_in, local_mix)


def rest_kernel(start, state_ref, mix_ref, after_ref, out_ref):
    pairs = state_ref.shape[0]
    for p in range(out_ref.shape[0]):
        pair = start + p
        other = state_ref[pair ^ pairs // 2]
        mixed = mix_pair(state_ref[pair], other, mix_ref[2 * pair : 2 * pair + 2])
        out_ref[p] = mixed.astype(out_ref.dtype)


def local_rest(state, last_mix, start, stop, after):
    _, rank, lanes = state.shape
    return pl.pallas_call(
        functools.partial(rest_kernel, start),
        out_shape=pltpu.VMEM((stop - start, rank, lanes), state.dtype),
        in_specs=[pl.BlockSpec(memory_space=pltpu.VMEM)] * 2 + [pl.BlockSpec(memory_space=pl.ANY)],
        out_specs=pl.BlockSpec(memory_space=pltpu.VMEM),
        compiler_params=pltpu.CompilerParams(vmem_limit_bytes=8 << 20),
        cost_estimate=pl.CostEstimate(flops=3 * 10**9, bytes_accessed=0, transcendentals=0),
        name="local_rest",
    )(state, last_mix, after)


def cross_kernel(level, start, offset, own_ref, other_ref, mix_ref, after_ref, out_ref):
    for p in range(out_ref.shape[0]):
        block = 2 * (start + p)
        mixed = mix_pair(
            own_ref[offset + p], other_ref[offset + p], mix_ref[block : block + 2, level]
        )
        out_ref[p] = mixed.astype(out_ref.dtype)


def cross_level(own, other, mix, level, start, offset, size, after):
    _, rank, lanes = own.shape
    return pl.pallas_call(
        functools.partial(cross_kernel, level, start, offset),
        out_shape=pltpu.VMEM((size, rank, lanes), own.dtype),
        in_specs=[pl.BlockSpec(memory_space=pltpu.VMEM)] * 3 + [pl.BlockSpec(memory_space=pl.ANY)],
        out_specs=pl.BlockSpec(memory_space=pltpu.VMEM),
        compiler_params=pltpu.CompilerParams(vmem_limit_bytes=8 << 20),
        cost_estimate=pl.CostEstimate(flops=3 * 10**9, bytes_accessed=0, transcendentals=0),
        name="cross_level",
    )(own, other, mix, after)


def final_kernel(has_token, level, start, own_ref, other_ref, mix_ref, leaf_ref, *rest):
    out_hbm, *tokens, held, sem = rest[-4 if has_token else -3 :]
    for token in tokens:
        token[...] = jnp.zeros_like(token)
    pairs = own_ref.shape[0]
    vectors = held.shape[0]
    width = leaf_ref.shape[2]
    turned = []
    for p in range(pairs):
        block = 2 * (start + p)
        mixed = mix_pair(own_ref[p], other_ref[p], mix_ref[block : block + 2, level])
        turned.append(mixed.astype(jnp.bfloat16).T)
    copies = []
    for first, stop in ((0, pairs // 2), (pairs // 2, pairs)):
        for p in range(first, stop):
            for side in range(2):
                held[:, pl.ds((2 * p + side) * width, width)] = jnp.dot(
                    turned[p][side * vectors : (side + 1) * vectors],
                    leaf_ref[2 * (start + p) + side],
                    preferred_element_type=jnp.float32,
                ).astype(held.dtype)
        count = 2 * (stop - first) * width
        copies.append(
            pltpu.make_async_copy(
                held.at[:, pl.ds(2 * first * width, count)],
                out_hbm.at[:, pl.ds(2 * (start + first) * width, count)],
                sem.at[len(copies)],
            )
        )
        copies[-1].start()
    for copy in copies:
        copy.wait()


def final_level(own, other, mix, leaf_out, level, start, so_far, after, has_token):
    blocks, rank, width = leaf_out.shape
    pairs, _, lanes = own.shape
    vectors = lanes // 2
    in_specs = [pl.BlockSpec(memory_space=pltpu.VMEM)] * 4 + [pl.BlockSpec(memory_space=pl.ANY)]
    operands = [own, other, mix, leaf_out, after]
    aliases = {}
    if so_far is not None:
        in_specs.append(pl.BlockSpec(memory_space=pltpu.HBM))
        operands.append(so_far)
        aliases = {5: 0}
    return pl.pallas_call(
        functools.partial(final_kernel, has_token, level, start),
        out_shape=[jax.ShapeDtypeStruct((vectors, blocks * width), own.dtype)]
        + [pltpu.VMEM((8, lanes), jnp.float32)] * has_token,
        in_specs=in_specs,
        out_specs=[pl.BlockSpec(memory_space=pltpu.HBM)]
        + [pl.BlockSpec(memory_space=pltpu.VMEM)] * has_token,
        scratch_shapes=[
            pltpu.VMEM((vectors, 2 * pairs * width), own.dtype),
            pltpu.SemaphoreType.DMA((2,)),
        ],
        input_output_aliases=aliases,
        compiler_params=pltpu.CompilerParams(vmem_limit_bytes=8 << 20),
        cost_estimate=pl.CostEstimate(flops=3 * 10**9, bytes_accessed=0, transcendentals=0),
        name="final_level",
    )(*operands)


def swapped(block, axis, stride):
    count = lax.axis_size(axis)
    route = [(i, i ^ (1 << stride)) for i in range(count)]
    return lax.ppermute(block, axis, route)


def cut(total, shares):
    ends = [total * sum(shares[: c + 1]) // sum(shares) for c in range(len(shares))]
    return list(zip([0] + ends[:-1], ends))


def body(sources, leaf_in, local_mix, lo_mix, hi_mix, leaf_out):
    lo_levels = lax.axis_size("lo").bit_length() - 1
    hi_levels = lax.axis_size("hi").bit_length() - 1
    pairs = leaf_in.shape[0] // 2
    steps = [("lo", n, lo_mix) for n in range(lo_levels)]
    steps += [("hi", n, hi_mix) for n in range(hi_levels)]
    end = len(steps) - 1
    parts = cut(pairs, SHARES)
    head = parts[0][1]
    waiting = {}

    def turn(item):
        s, c = item
        lags = LAGS[min(end - s, 3) if s else 4]
        return s + lags[c], -s

    first, state, last_mix = local_phase(sources, leaf_in, local_mix, head)
    axis, level, _ = steps[0]
    waiting[0, 0] = first, swapped(first, axis, level), 0
    after = state
    targets = None
    for s, c in sorted(((s, c) for s in range(end + 1) for c in range(len(parts))), key=turn):
        own, other, offset = waiting.pop((s, c))
        _, level, mix = steps[s]
        start, stop = parts[c]
        if s == end:
            more = c < len(parts) - 1
            targets, *tokens = final_level(
                own, other, mix, leaf_out, level, start, targets, after, more
            )
            after = tokens[0] if more else None
            continue
        block = after = cross_level(own, other, mix, level, start, offset, stop - start, after)
        if s == 0 and c == 0:
            after = local_rest(state, last_mix, *parts[1], after)
            waiting[0, 1] = after, swapped(after, *steps[0][:2]), 0
        if s == 0 and c == 1:
            after = rest = local_rest(state, last_mix, stop, pairs, after)
            partner = swapped(rest, *steps[0][:2])
            for d in range(2, len(parts)):
                waiting[0, d] = rest, partner, parts[d][0] - stop
        axis, level, _ = steps[s + 1]
        waiting[s + 1, c] = block, swapped(block, axis, level), 0
    return targets


def solution(mesh):
    return jax.shard_map(
        body,
        mesh=mesh,
        in_specs=(
            P(None, ("hi", "lo")),
            P(("hi", "lo"), None, None),
            P(("hi", "lo"), None, None, None),
            P(("hi", "lo"), None, None, None),
            P(("hi", "lo"), None, None, None),
            P(("hi", "lo"), None, None),
        ),
        out_specs=P(None, ("hi", "lo")),
        check_vma=False,
    )
```

```python
import functools

import jax
import jax.numpy as jnp
from jax import lax
from jax.experimental import pallas as pl
from jax.experimental.pallas import tpu as pltpu
from jax.sharding import PartitionSpec as P

NT = (((1,), (1,)), ((), ()))
PIECES = 4
SHARES = (5, 8, 10, 9)
LAGS = (
    (1.0, 1.1, 1.2, 1.3),
    (0.0, 0.5, 1.2, 1.6),
    (0.0, 0.5, 1.1, 1.6),
    (0.0, 0.5, 1.2, 2.15),
    (0.0, 0.9, 1.1, 2.1),
)


def half_swap(x):
    half = x.shape[1] // 2
    return jnp.concatenate([x[:, half:], x[:, :half]], axis=1)


def pack(product):
    rows = product.shape[0] // 2
    top, bottom = product[:rows], product[rows:]
    low = lax.broadcasted_iota(jnp.int32, top.shape, 1) < top.shape[1] // 2
    return jnp.where(low, top, bottom)


def mix_pair(own, other, factors):
    joined = jnp.concatenate([own, other], axis=0)
    rows, width = factors.shape[1:]
    product = jnp.dot(
        factors.reshape(2 * rows, width), joined, preferred_element_type=jnp.float32
    )
    return pack(product)


def local_kernel(
    src_hbm,
    leaf_hbm,
    mix_hbm,
    lo_hbm,
    first,
    state,
    last_mix,
    lo_head,
    even,
    odd,
    src,
    leaf,
    mix,
    src_sem,
    leaf_sem,
    mix_sem,
    lo_sem,
):
    pairs = even.shape[0]
    blocks = leaf.shape[0]
    levels = mix_hbm.shape[1]
    width = leaf.shape[2]

    def inputs(piece):
        count = blocks // PIECES
        cols = pl.ds(piece * count * width, count * width)
        rows = pl.ds(piece * count, count)
        return (
            pltpu.make_async_copy(src_hbm.at[:, cols], src.at[:, cols], src_sem.at[piece]),
            pltpu.make_async_copy(leaf_hbm.at[rows], leaf.at[rows], leaf_sem.at[piece]),
        )

    def factors(level):
        held = mix.at[level] if level < levels - 1 else last_mix
        return pltpu.make_async_copy(mix_hbm.at[:, level], held, mix_sem.at[level])

    for piece in range(PIECES):
        for copy in inputs(piece):
            copy.start()

    head = pl.ds(0, lo_head.shape[0])
    next_level = pltpu.make_async_copy(lo_hbm.at[head, pl.ds(0, 1)], lo_head, lo_sem)
    queue = [factors(level) for level in range(levels)]
    for piece in range(PIECES):
        for copy in inputs(piece):
            copy.wait()
        for copy in queue[piece * levels // PIECES : (piece + 1) * levels // PIECES]:
            copy.start()
        for pair in range(piece * pairs // PIECES, (piece + 1) * pairs // PIECES):
            columns = [src[:, pl.ds((2 * pair + side) * width, width)] for side in range(2)]
            product = lax.dot_general(
                leaf[2 * pair : 2 * pair + 2].reshape(-1, width),
                jnp.concatenate(columns, axis=0),
                NT,
                preferred_element_type=jnp.float32,
            )
            even[pair] = pack(product).astype(even.dtype)

    next_level.start()

    for level in range(levels):
        factors(level).wait()
        old, new = (odd, even) if level % 2 else (even, odd)
        if level == levels - 2:
            new = state
        if level == levels - 1:
            old, new = state, first
        for pair in range(new.shape[0]):
            own = old[pair]
            other = half_swap(own) if level == 0 else old[pair ^ 1 << level - 1]
            chosen = last_mix if level == levels - 1 else mix.at[level]
            part = chosen[2 * pair : 2 * pair + 2]
            new[pair] = mix_pair(own, other, part).astype(own.dtype)
    next_level.wait()


def local_phase(sources, leaf_in, local_mix, lo_mix, size, blocks_next):
    vectors = sources.shape[0]
    blocks, rank, _ = leaf_in.shape
    levels = local_mix.shape[1]
    return pl.pallas_call(
        local_kernel,
        out_shape=[
            pltpu.VMEM((size, rank, 2 * vectors), jnp.bfloat16),
            pltpu.VMEM((blocks // 2, rank, 2 * vectors), jnp.bfloat16),
            pltpu.VMEM((blocks,) + local_mix.shape[2:], local_mix.dtype),
            pltpu.VMEM((blocks_next, 1) + lo_mix.shape[2:], lo_mix.dtype),
        ],
        in_specs=[pl.BlockSpec(memory_space=pltpu.HBM)] * 4,
        out_specs=[pl.BlockSpec(memory_space=pltpu.VMEM)] * 4,
        scratch_shapes=[
            pltpu.VMEM((blocks // 2, rank, 2 * vectors), jnp.bfloat16),
            pltpu.VMEM((blocks // 2, rank, 2 * vectors), jnp.bfloat16),
            pltpu.VMEM(sources.shape, sources.dtype),
            pltpu.VMEM(leaf_in.shape, leaf_in.dtype),
            pltpu.VMEM((levels - 1, blocks) + local_mix.shape[2:], local_mix.dtype),
            pltpu.SemaphoreType.DMA((PIECES,)),
            pltpu.SemaphoreType.DMA((PIECES,)),
            pltpu.SemaphoreType.DMA((levels,)),
            pltpu.SemaphoreType.DMA,
        ],
        compiler_params=pltpu.CompilerParams(vmem_limit_bytes=58 << 20),
        cost_estimate=pl.CostEstimate(flops=10**9, bytes_accessed=10 << 20, transcendentals=0),
        name="local_levels",
    )(sources, leaf_in, local_mix, lo_mix)


def rest_kernel(start, state_ref, mix_ref, after_ref, out_ref):
    pairs = state_ref.shape[0]
    for p in range(out_ref.shape[0]):
        pair = start + p
        other = state_ref[pair ^ pairs // 2]
        mixed = mix_pair(state_ref[pair], other, mix_ref[2 * pair : 2 * pair + 2])
        out_ref[p] = mixed.astype(out_ref.dtype)


def local_rest(state, last_mix, start, stop, after):
    _, rank, lanes = state.shape
    return pl.pallas_call(
        functools.partial(rest_kernel, start),
        out_shape=pltpu.VMEM((stop - start, rank, lanes), state.dtype),
        in_specs=[pl.BlockSpec(memory_space=pltpu.VMEM)] * 2 + [pl.BlockSpec(memory_space=pl.ANY)],
        out_specs=pl.BlockSpec(memory_space=pltpu.VMEM),
        compiler_params=pltpu.CompilerParams(vmem_limit_bytes=8 << 20),
        cost_estimate=pl.CostEstimate(flops=3 * 10**9, bytes_accessed=0, transcendentals=0),
        name="local_rest",
    )(state, last_mix, after)


def cross_kernel(level, start, offset, own_ref, other_ref, mix_ref, after_ref, out_ref):
    for p in range(out_ref.shape[0]):
        block = 2 * (start + p)
        mixed = mix_pair(
            own_ref[offset + p], other_ref[offset + p], mix_ref[block : block + 2, level]
        )
        out_ref[p] = mixed.astype(out_ref.dtype)


def cross_level(own, other, mix, level, start, offset, size, after):
    _, rank, lanes = own.shape
    return pl.pallas_call(
        functools.partial(cross_kernel, level, start, offset),
        out_shape=pltpu.VMEM((size, rank, lanes), own.dtype),
        in_specs=[pl.BlockSpec(memory_space=pltpu.VMEM)] * 3 + [pl.BlockSpec(memory_space=pl.ANY)],
        out_specs=pl.BlockSpec(memory_space=pltpu.VMEM),
        compiler_params=pltpu.CompilerParams(vmem_limit_bytes=8 << 20),
        cost_estimate=pl.CostEstimate(flops=3 * 10**9, bytes_accessed=0, transcendentals=0),
        name="cross_level",
    )(own, other, mix, after)


def final_kernel(has_token, level, start, own_ref, other_ref, mix_ref, leaf_ref, *rest):
    out_hbm, *tokens, held, sem = rest[-4 if has_token else -3 :]
    for token in tokens:
        token[...] = jnp.zeros_like(token)
    pairs = own_ref.shape[0]
    vectors = held.shape[0]
    width = leaf_ref.shape[2]
    turned = []
    for p in range(pairs):
        block = 2 * (start + p)
        mixed = mix_pair(own_ref[p], other_ref[p], mix_ref[block : block + 2, level])
        turned.append(mixed.astype(jnp.bfloat16).T)
    copies = []
    for first, stop in ((0, pairs // 2), (pairs // 2, pairs)):
        for p in range(first, stop):
            for side in range(2):
                held[:, pl.ds((2 * p + side) * width, width)] = jnp.dot(
                    turned[p][side * vectors : (side + 1) * vectors],
                    leaf_ref[2 * (start + p) + side],
                    preferred_element_type=jnp.float32,
                ).astype(held.dtype)
        count = 2 * (stop - first) * width
        copies.append(
            pltpu.make_async_copy(
                held.at[:, pl.ds(2 * first * width, count)],
                out_hbm.at[:, pl.ds(2 * (start + first) * width, count)],
                sem.at[len(copies)],
            )
        )
        copies[-1].start()
    for copy in copies:
        copy.wait()


def final_level(own, other, mix, leaf_out, level, start, so_far, after, has_token):
    blocks, rank, width = leaf_out.shape
    pairs, _, lanes = own.shape
    vectors = lanes // 2
    in_specs = [pl.BlockSpec(memory_space=pltpu.VMEM)] * 4 + [pl.BlockSpec(memory_space=pl.ANY)]
    operands = [own, other, mix, leaf_out, after]
    aliases = {}
    if so_far is not None:
        in_specs.append(pl.BlockSpec(memory_space=pltpu.HBM))
        operands.append(so_far)
        aliases = {5: 0}
    return pl.pallas_call(
        functools.partial(final_kernel, has_token, level, start),
        out_shape=[jax.ShapeDtypeStruct((vectors, blocks * width), own.dtype)]
        + [pltpu.VMEM((8, lanes), jnp.float32)] * has_token,
        in_specs=in_specs,
        out_specs=[pl.BlockSpec(memory_space=pltpu.HBM)]
        + [pl.BlockSpec(memory_space=pltpu.VMEM)] * has_token,
        scratch_shapes=[
            pltpu.VMEM((vectors, 2 * pairs * width), own.dtype),
            pltpu.SemaphoreType.DMA((2,)),
        ],
        input_output_aliases=aliases,
        compiler_params=pltpu.CompilerParams(vmem_limit_bytes=8 << 20),
        cost_estimate=pl.CostEstimate(flops=3 * 10**9, bytes_accessed=0, transcendentals=0),
        name="final_level",
    )(*operands)


def swapped(block, axis, stride):
    count = lax.axis_size(axis)
    route = [(i, i ^ (1 << stride)) for i in range(count)]
    return lax.ppermute(block, axis, route)


def cut(total, shares):
    ends = [total * sum(shares[: c + 1]) // sum(shares) for c in range(len(shares))]
    return list(zip([0] + ends[:-1], ends))


def body(sources, leaf_in, local_mix, lo_mix, hi_mix, leaf_out):
    lo_levels = lax.axis_size("lo").bit_length() - 1
    hi_levels = lax.axis_size("hi").bit_length() - 1
    pairs = leaf_in.shape[0] // 2
    steps = [("lo", n, lo_mix) for n in range(lo_levels)]
    steps += [("hi", n, hi_mix) for n in range(hi_levels)]
    end = len(steps) - 1
    parts = cut(pairs, SHARES)
    head = parts[0][1]
    waiting = {}

    def turn(item):
        s, c = item
        lags = LAGS[min(end - s, 3) if s else 4]
        return s + lags[c], -s

    first, state, last_mix, lo_head = local_phase(
        sources, leaf_in, local_mix, lo_mix, head, 2 * parts[1][1]
    )
    axis, level, _ = steps[0]
    waiting[0, 0] = first, swapped(first, axis, level), 0
    after = state
    targets = None
    for s, c in sorted(((s, c) for s in range(end + 1) for c in range(len(parts))), key=turn):
        own, other, offset = waiting.pop((s, c))
        _, level, mix = steps[s]
        if s == 0 and c < 2:
            mix = lo_head
        start, stop = parts[c]
        if s == end:
            more = c < len(parts) - 1
            targets, *tokens = final_level(
                own, other, mix, leaf_out, level, start, targets, after, more
            )
            after = tokens[0] if more else None
            continue
        block = after = cross_level(own, other, mix, level, start, offset, stop - start, after)
        if s == 0 and c == 0:
            after = local_rest(state, last_mix, *parts[1], after)
            waiting[0, 1] = after, swapped(after, *steps[0][:2]), 0
        if s == 0 and c == 1:
            after = rest = local_rest(state, last_mix, stop, pairs, after)
            partner = swapped(rest, *steps[0][:2])
            for d in range(2, len(parts)):
                waiting[0, d] = rest, partner, parts[d][0] - stop
        axis, level, _ = steps[s + 1]
        waiting[s + 1, c] = block, swapped(block, axis, level), 0
    return targets


def solution(mesh):
    return jax.shard_map(
        body,
        mesh=mesh,
        in_specs=(
            P(None, ("hi", "lo")),
            P(("hi", "lo"), None, None),
            P(("hi", "lo"), None, None, None),
            P(("hi", "lo"), None, None, None),
            P(("hi", "lo"), None, None, None),
            P(("hi", "lo"), None, None),
        ),
        out_specs=P(None, ("hi", "lo")),
        check_vma=False,
    )
```

```python
import functools

import jax
import jax.numpy as jnp
from jax import lax
from jax.experimental import pallas as pl
from jax.experimental.pallas import tpu as pltpu
from jax.sharding import PartitionSpec as P

NT = (((1,), (1,)), ((), ()))
PIECES = 4
SHARES = (4, 9, 10, 9)
LAGS = (
    (1.0, 1.1, 1.2, 1.3),
    (0.0, 0.5, 1.2, 1.6),
    (0.0, 0.5, 1.1, 1.6),
    (0.0, 0.5, 1.2, 2.15),
    (0.0, 0.9, 1.1, 2.1),
)


def half_swap(x):
    half = x.shape[1] // 2
    return jnp.concatenate([x[:, half:], x[:, :half]], axis=1)


def pack(product):
    rows = product.shape[0] // 2
    top, bottom = product[:rows], product[rows:]
    low = lax.broadcasted_iota(jnp.int32, top.shape, 1) < top.shape[1] // 2
    return jnp.where(low, top, bottom)


def mix_pair(own, other, factors):
    joined = jnp.concatenate([own, other], axis=0)
    rows, width = factors.shape[1:]
    product = jnp.dot(
        factors.reshape(2 * rows, width), joined, preferred_element_type=jnp.float32
    )
    return pack(product)


def local_kernel(
    src_hbm,
    leaf_hbm,
    mix_hbm,
    lo_hbm,
    first,
    second,
    state,
    last_mix,
    lo_head,
    even,
    odd,
    src,
    leaf,
    mix,
    src_sem,
    leaf_sem,
    mix_sem,
    lo_sem,
):
    pairs = even.shape[0]
    blocks = leaf.shape[0]
    levels = mix_hbm.shape[1]
    width = leaf.shape[2]

    def inputs(piece):
        count = blocks // PIECES
        cols = pl.ds(piece * count * width, count * width)
        rows = pl.ds(piece * count, count)
        return (
            pltpu.make_async_copy(src_hbm.at[:, cols], src.at[:, cols], src_sem.at[piece]),
            pltpu.make_async_copy(leaf_hbm.at[rows], leaf.at[rows], leaf_sem.at[piece]),
        )

    def factors(level):
        held = mix.at[level] if level < levels - 1 else last_mix
        return pltpu.make_async_copy(mix_hbm.at[:, level], held, mix_sem.at[level])

    for piece in range(PIECES):
        for copy in inputs(piece):
            copy.start()

    head = pl.ds(0, lo_head.shape[0])
    next_level = pltpu.make_async_copy(lo_hbm.at[head, pl.ds(0, 1)], lo_head, lo_sem)
    queue = [factors(level) for level in range(levels)]
    for piece in range(PIECES):
        for copy in inputs(piece):
            copy.wait()
        for copy in queue[piece * levels // PIECES : (piece + 1) * levels // PIECES]:
            copy.start()
        for pair in range(piece * pairs // PIECES, (piece + 1) * pairs // PIECES):
            columns = [src[:, pl.ds((2 * pair + side) * width, width)] for side in range(2)]
            product = lax.dot_general(
                leaf[2 * pair : 2 * pair + 2].reshape(-1, width),
                jnp.concatenate(columns, axis=0),
                NT,
                preferred_element_type=jnp.float32,
            )
            even[pair] = pack(product).astype(even.dtype)

    next_level.start()

    for level in range(levels):
        factors(level).wait()
        old, new = (odd, even) if level % 2 else (even, odd)
        if level == levels - 2:
            new = state
        count = pairs
        if level == levels - 1:
            old = state
            count = first.shape[0] + second.shape[0]
        for pair in range(count):
            own = old[pair]
            other = half_swap(own) if level == 0 else old[pair ^ 1 << level - 1]
            chosen = last_mix if level == levels - 1 else mix.at[level]
            part = chosen[2 * pair : 2 * pair + 2]
            mixed = mix_pair(own, other, part).astype(own.dtype)
            if level < levels - 1:
                new[pair] = mixed
            elif pair < first.shape[0]:
                first[pair] = mixed
            else:
                second[pair - first.shape[0]] = mixed
    next_level.wait()


def local_phase(sources, leaf_in, local_mix, lo_mix, sizes):
    vectors = sources.shape[0]
    blocks, rank, _ = leaf_in.shape
    levels = local_mix.shape[1]
    return pl.pallas_call(
        local_kernel,
        out_shape=[pltpu.VMEM((n, rank, 2 * vectors), jnp.bfloat16) for n in sizes]
        + [
            pltpu.VMEM((blocks // 2, rank, 2 * vectors), jnp.bfloat16),
            pltpu.VMEM((blocks,) + local_mix.shape[2:], local_mix.dtype),
            pltpu.VMEM((2 * sum(sizes), 1) + lo_mix.shape[2:], lo_mix.dtype),
        ],
        in_specs=[pl.BlockSpec(memory_space=pltpu.HBM)] * 4,
        out_specs=[pl.BlockSpec(memory_space=pltpu.VMEM)] * 5,
        scratch_shapes=[
            pltpu.VMEM((blocks // 2, rank, 2 * vectors), jnp.bfloat16),
            pltpu.VMEM((blocks // 2, rank, 2 * vectors), jnp.bfloat16),
            pltpu.VMEM(sources.shape, sources.dtype),
            pltpu.VMEM(leaf_in.shape, leaf_in.dtype),
            pltpu.VMEM((levels - 1, blocks) + local_mix.shape[2:], local_mix.dtype),
            pltpu.SemaphoreType.DMA((PIECES,)),
            pltpu.SemaphoreType.DMA((PIECES,)),
            pltpu.SemaphoreType.DMA((levels,)),
            pltpu.SemaphoreType.DMA,
        ],
        compiler_params=pltpu.CompilerParams(vmem_limit_bytes=58 << 20),
        cost_estimate=pl.CostEstimate(flops=10**9, bytes_accessed=10 << 20, transcendentals=0),
        name="local_levels",
    )(sources, leaf_in, local_mix, lo_mix)


def rest_kernel(start, state_ref, mix_ref, after_ref, out_ref):
    pairs = state_ref.shape[0]
    for p in range(out_ref.shape[0]):
        pair = start + p
        other = state_ref[pair ^ pairs // 2]
        mixed = mix_pair(state_ref[pair], other, mix_ref[2 * pair : 2 * pair + 2])
        out_ref[p] = mixed.astype(out_ref.dtype)


def local_rest(state, last_mix, start, stop, after):
    _, rank, lanes = state.shape
    return pl.pallas_call(
        functools.partial(rest_kernel, start),
        out_shape=pltpu.VMEM((stop - start, rank, lanes), state.dtype),
        in_specs=[pl.BlockSpec(memory_space=pltpu.VMEM)] * 2 + [pl.BlockSpec(memory_space=pl.ANY)],
        out_specs=pl.BlockSpec(memory_space=pltpu.VMEM),
        compiler_params=pltpu.CompilerParams(vmem_limit_bytes=8 << 20),
        cost_estimate=pl.CostEstimate(flops=3 * 10**9, bytes_accessed=0, transcendentals=0),
        name="local_rest",
    )(state, last_mix, after)


def cross_kernel(level, start, offset, own_ref, other_ref, mix_ref, after_ref, out_ref):
    for p in range(out_ref.shape[0]):
        block = 2 * (start + p)
        mixed = mix_pair(
            own_ref[offset + p], other_ref[offset + p], mix_ref[block : block + 2, level]
        )
        out_ref[p] = mixed.astype(out_ref.dtype)


def cross_level(own, other, mix, level, start, offset, size, after):
    _, rank, lanes = own.shape
    return pl.pallas_call(
        functools.partial(cross_kernel, level, start, offset),
        out_shape=pltpu.VMEM((size, rank, lanes), own.dtype),
        in_specs=[pl.BlockSpec(memory_space=pltpu.VMEM)] * 3 + [pl.BlockSpec(memory_space=pl.ANY)],
        out_specs=pl.BlockSpec(memory_space=pltpu.VMEM),
        compiler_params=pltpu.CompilerParams(vmem_limit_bytes=8 << 20),
        cost_estimate=pl.CostEstimate(flops=3 * 10**9, bytes_accessed=0, transcendentals=0),
        name="cross_level",
    )(own, other, mix, after)


def final_kernel(has_token, level, start, own_ref, other_ref, mix_ref, leaf_ref, *rest):
    out_hbm, *tokens, held, sem = rest[-4 if has_token else -3 :]
    for token in tokens:
        token[...] = jnp.zeros_like(token)
    pairs = own_ref.shape[0]
    vectors = held.shape[0]
    width = leaf_ref.shape[2]
    turned = []
    for p in range(pairs):
        block = 2 * (start + p)
        mixed = mix_pair(own_ref[p], other_ref[p], mix_ref[block : block + 2, level])
        turned.append(mixed.astype(jnp.bfloat16).T)
    copies = []
    for first, stop in ((0, pairs // 2), (pairs // 2, pairs)):
        for p in range(first, stop):
            for side in range(2):
                held[:, pl.ds((2 * p + side) * width, width)] = jnp.dot(
                    turned[p][side * vectors : (side + 1) * vectors],
                    leaf_ref[2 * (start + p) + side],
                    preferred_element_type=jnp.float32,
                ).astype(held.dtype)
        count = 2 * (stop - first) * width
        copies.append(
            pltpu.make_async_copy(
                held.at[:, pl.ds(2 * first * width, count)],
                out_hbm.at[:, pl.ds(2 * (start + first) * width, count)],
                sem.at[len(copies)],
            )
        )
        copies[-1].start()
    for copy in copies:
        copy.wait()


def final_level(own, other, mix, leaf_out, level, start, so_far, after, has_token):
    blocks, rank, width = leaf_out.shape
    pairs, _, lanes = own.shape
    vectors = lanes // 2
    in_specs = [pl.BlockSpec(memory_space=pltpu.VMEM)] * 4 + [pl.BlockSpec(memory_space=pl.ANY)]
    operands = [own, other, mix, leaf_out, after]
    aliases = {}
    if so_far is not None:
        in_specs.append(pl.BlockSpec(memory_space=pltpu.HBM))
        operands.append(so_far)
        aliases = {5: 0}
    return pl.pallas_call(
        functools.partial(final_kernel, has_token, level, start),
        out_shape=[jax.ShapeDtypeStruct((vectors, blocks * width), own.dtype)]
        + [pltpu.VMEM((8, lanes), jnp.float32)] * has_token,
        in_specs=in_specs,
        out_specs=[pl.BlockSpec(memory_space=pltpu.HBM)]
        + [pl.BlockSpec(memory_space=pltpu.VMEM)] * has_token,
        scratch_shapes=[
            pltpu.VMEM((vectors, 2 * pairs * width), own.dtype),
            pltpu.SemaphoreType.DMA((2,)),
        ],
        input_output_aliases=aliases,
        compiler_params=pltpu.CompilerParams(vmem_limit_bytes=8 << 20),
        cost_estimate=pl.CostEstimate(flops=3 * 10**9, bytes_accessed=0, transcendentals=0),
        name="final_level",
    )(*operands)


def swapped(block, axis, stride):
    count = lax.axis_size(axis)
    route = [(i, i ^ (1 << stride)) for i in range(count)]
    return lax.ppermute(block, axis, route)


def cut(total, shares):
    ends = [total * sum(shares[: c + 1]) // sum(shares) for c in range(len(shares))]
    return list(zip([0] + ends[:-1], ends))


def body(sources, leaf_in, local_mix, lo_mix, hi_mix, leaf_out):
    lo_levels = lax.axis_size("lo").bit_length() - 1
    hi_levels = lax.axis_size("hi").bit_length() - 1
    pairs = leaf_in.shape[0] // 2
    steps = [("lo", n, lo_mix) for n in range(lo_levels)]
    steps += [("hi", n, hi_mix) for n in range(hi_levels)]
    end = len(steps) - 1
    parts = cut(pairs, SHARES)
    waiting = {}

    def turn(item):
        s, c = item
        lags = LAGS[min(end - s, 3) if s else 4]
        return s + lags[c], -s

    *blocks, state, last_mix, lo_head = local_phase(
        sources, leaf_in, local_mix, lo_mix, [stop - start for start, stop in parts[:2]]
    )
    for c, block in enumerate(blocks):
        waiting[0, c] = block, swapped(block, *steps[0][:2]), 0
    after = state
    targets = None
    for s, c in sorted(((s, c) for s in range(end + 1) for c in range(len(parts))), key=turn):
        own, other, offset = waiting.pop((s, c))
        _, level, mix = steps[s]
        if s == 0 and c < 2:
            mix = lo_head
        start, stop = parts[c]
        if s == end:
            more = c < len(parts) - 1
            targets, *tokens = final_level(
                own, other, mix, leaf_out, level, start, targets, after, more
            )
            after = tokens[0] if more else None
            continue
        block = after = cross_level(own, other, mix, level, start, offset, stop - start, after)
        if s == 0 and c == 1:
            after = rest = local_rest(state, last_mix, stop, pairs, after)
            partner = swapped(rest, *steps[0][:2])
            for d in range(2, len(parts)):
                waiting[0, d] = rest, partner, parts[d][0] - stop
        axis, level, _ = steps[s + 1]
        waiting[s + 1, c] = block, swapped(block, axis, level), 0
    return targets


def solution(mesh):
    return jax.shard_map(
        body,
        mesh=mesh,
        in_specs=(
            P(None, ("hi", "lo")),
            P(("hi", "lo"), None, None),
            P(("hi", "lo"), None, None, None),
            P(("hi", "lo"), None, None, None),
            P(("hi", "lo"), None, None, None),
            P(("hi", "lo"), None, None),
        ),
        out_specs=P(None, ("hi", "lo")),
        check_vma=False,
    )
```
